512 devices in a mesh: tm: 32 (over x, y, core), tile: 16 (over z).
Axes of the slice: x: 4, y: 4, z: 16, core: 2. Of those that a mesh axis runs over, the one named last changes fastest.
Arguments:
- seg_gain: bfloat16 [32, 1024, 1024], P('tm', 'tile'), may hold values from -0.1875 to 0.1875
- seg_offset: float32 [32, 1024], P('tm', 'tile'), may hold values from -6 to 6
- seg_noise: bfloat16 [32, 1024, 1024], P('tm', 'tile'), as said below
- end_mean: bfloat16 [8, 1024], P(None, 'tile'), may hold values from -6 to 6
- end_cov: bfloat16 [8, 1024, 1024], P(None, 'tile'), as said below
- step_gain: bfloat16 [256, 1024, 1024], P('tm', 'tile'), may hold values from -0.1875 to 0.1875
- step_offset: float32 [256, 1024], P('tm', 'tile'), may hold values from -6 to 6
- step_var: float32 [256, 1024], P('tm', 'tile'), may hold values from 0.1 to 1.5
- obs_tiles: int32 [256, 4], P('tm'), may hold values from 0 to 7
- obs_count: int32 [256], P('tm'), may hold values from 1 to 4, as said below
- obs_value: float32 [256, 4, 128], P('tm'), may hold values from -10 to 10
- obs_noise: float32 [1024], replicated, may hold values from 0.2 to 2
Outputs:
- start_cov: bfloat16 [32, 1024, 1024], P('tm', 'tile')
- start_mean: bfloat16 [32, 1024], P('tm', 'tile')
- step_mean: float32 [256, 1024], P('tm', 'tile')
- step_spread: float32 [256, 1024], P('tm', 'tile')
- innovation: float32 [256, 4, 128], P('tm')
The draws below stay inside these ranges and needn't reach their ends.
Inputs may be any that keep to these rules, and one draw needn't show every extreme that they name: `end_cov`: each matrix is symmetric and positive definite. `seg_noise`: each matrix is symmetric and positive definite. `obs_count`: some step has 4 live slots and some has 1.
All inputs are finite; a program needn't handle non-finite values.
Results may differ from the reference program's by a relative error of at most 0.015.
Values may be sent and summed in bfloat16 or wider, within the bound.
A program may use at most 64 MiB of HBM per device.

```python
import math
import jax
import jax.numpy as jnp
from jax import lax

D = 1024
STEPS_SEG = 8
TILE_STATES = 128
SLOTS = 4
GROUP_SEGS = 4
SEGS = 32
GROUPS = 8
STEPS = 256
NTILES = 8


def correlated_blocks(key, count, amp_low, amp_high, diag_low, diag_high, length, reach, mixing):
    first_key, second_key, third_key, fourth_key = jax.random.split(key, 4)
    amplitude = jax.random.uniform(first_key, (count, D), jnp.float32, amp_low, amp_high)
    places = jnp.arange(D, dtype=jnp.float32)
    distance = jnp.abs(places[:, None] - places[None, :])
    kernel = jnp.exp(-distance / length)
    smooth = amplitude[:, :, None] * amplitude[:, None, :] * kernel[None, :, :]
    raw = jax.random.uniform(second_key, (count, D, D), jnp.float32, -1.0, 1.0) * (reach / D)
    paired = raw + jnp.swapaxes(raw, 1, 2)
    diagonal = jax.random.uniform(third_key, (count, D), jnp.float32, diag_low, diag_high)
    identity = jnp.eye(D, dtype=jnp.float32)
    result = smooth + paired * (1.0 - identity)[None, :, :] + identity[None, :, :] * diagonal[:, :, None]
    if mixing > 0.0:
        inner_width = D // 4
        factor = jax.random.normal(fourth_key, (count, D, inner_width), jnp.float32)
        wishart = jnp.einsum('gik,gjk->gij', factor, factor, precision=lax.Precision.HIGHEST)
        result = result + wishart * (mixing / inner_width)
    return result


def draw_end_cov(key, part):
    result = correlated_blocks(jax.random.fold_in(key, 11), GROUPS, 0.7, 1.5, 1.2, 2.0, D / 16.0, 0.5, 1.0)
    return result.astype(jnp.bfloat16)


def draw_seg_noise(key, part):
    result = correlated_blocks(jax.random.fold_in(key, 13), SEGS, 0.5, 1.2, 0.6, 1.4, D / 32.0, 0.2, 0.0)
    return result.astype(jnp.bfloat16)


def draw_obs_count(key, part):
    counts = jax.random.randint(jax.random.fold_in(key, 17), (STEPS,), 1, SLOTS + 1)
    counts = counts.at[0].set(SLOTS)
    counts = counts.at[1].set(1)
    return counts.astype(jnp.int32)


def touch_ends(drawn, rng, least, top_value):
    longest = drawn.shape.index(max(drawn.shape))
    spots = []
    for shift in (0, 1):
        where = [jax.random.randint(jax.random.fold_in(rng, axis), (), 0, length) for axis, length in enumerate(drawn.shape)]
        where[longest] = (where[longest] + shift) % drawn.shape[longest]
        spots.append(tuple(where))
    return drawn.at[spots[0]].set(least).at[spots[1]].set(top_value)


def block_scale(rng, shape, cuts, least, largest):
    def one(axis_at, shards_of):
        steps = jax.random.uniform(jax.random.fold_in(jax.random.fold_in(rng, 6), axis_at), (shards_of,), jnp.float32, least / len(cuts), largest / len(cuts))
        return jnp.repeat(jnp.exp(steps), shape[axis_at] // shards_of).reshape((-1,) + (1,) * (len(shape) - axis_at - 1))

    factor_of = one(*cuts[0])
    for cut in cuts[1:]:
        factor_of = factor_of * one(*cut)
    return factor_of


def bell_draw(key, dims, scale, limit, shards=(), kind=jnp.bfloat16):
    values = scale * jax.random.normal(key, dims, jnp.float32)
    if shards:
        values = values * block_scale(key, dims, shards, -0.22, 0.18)
    return jnp.clip(values, -limit, limit).astype(kind)


def setup_inputs(seed: int = 0) -> dict:
    key_of = jax.random.split(jax.random.key(seed), 13)
    return {
        "seg_gain": bell_draw(key_of[0], (SEGS, D, D), D ** -0.5, 0.1875, ((0, 32), (1, 16))),
        "seg_offset": bell_draw(key_of[1], (SEGS, D), 1.0, 6.0, ((0, 32), (1, 16)), jnp.float32),
        "seg_noise": draw_seg_noise(jax.random.fold_in(key_of[12], 71), 0),
        "end_mean": bell_draw(key_of[3], (GROUPS, D), 1.0, 6.0, ((1, 16),)),
        "end_cov": draw_end_cov(jax.random.fold_in(key_of[12], 71), 0),
        "step_gain": bell_draw(key_of[5], (STEPS, D, D), D ** -0.5, 0.1875, ((0, 32), (1, 16))),
        "step_offset": bell_draw(key_of[6], (STEPS, D), 1.0, 6.0, ((0, 32), (1, 16)), jnp.float32),
        "step_var": jnp.clip(jnp.exp(math.log(1.5) - 2.7080502 * jax.random.uniform(key_of[7], (STEPS, D), jnp.float32) ** block_scale(key_of[7], (STEPS, D), ((0, 32), (1, 16)), -0.2, 0.2)), 0.1, 1.5),
        "obs_tiles": touch_ends(jax.random.randint(key_of[8], (STEPS, SLOTS), 0, NTILES), jax.random.fold_in(key_of[8], 1), 0, NTILES - 1).astype(jnp.int32),
        "obs_count": draw_obs_count(jax.random.fold_in(key_of[12], 71), 0),
        "obs_value": bell_draw(key_of[10], (STEPS, SLOTS, TILE_STATES), 2.0, 10.0, ((0, 32),), jnp.float32),
        "obs_noise": jnp.clip(jnp.exp(jax.random.uniform(key_of[11], (D,), jnp.float32, math.log(0.2), math.log(2.0))), 0.2, 2.0),
    }


def apply_element(gain_mat, offset_vec, noise_mat, mean_vec, cov_mat):
    product = jnp.dot(gain_mat, cov_mat, preferred_element_type=jnp.float32).astype(jnp.bfloat16)
    new_cov = (jnp.dot(product, gain_mat.T, preferred_element_type=jnp.float32) + noise_mat.astype(jnp.float32)).astype(jnp.bfloat16)
    new_mean = (jnp.dot(gain_mat, mean_vec, preferred_element_type=jnp.float32) + offset_vec).astype(jnp.bfloat16)
    return new_mean, new_cov


def segment_moments(inputs):
    gains, offsets, variances, mean_vec, cov_mat = inputs
    gains_wide = gains.astype(jnp.float32)
    partial_value = jnp.einsum("kij,jl->kil", gains_wide, cov_mat.astype(jnp.float32), precision=lax.Precision.HIGHEST)
    spread = jnp.sum(partial_value * gains_wide, axis=2) + variances
    means = jnp.einsum("kij,j->ki", gains_wide, mean_vec.astype(jnp.float32), precision=lax.Precision.HIGHEST) + offsets
    return means, spread


def reference(seg_gain, seg_offset, seg_noise, end_mean, end_cov, step_gain, step_offset, step_var, obs_tiles, obs_count, obs_value, obs_noise):
    ends_mean = [None] * SEGS
    ends_cov = [None] * SEGS
    starts_mean = [None] * SEGS
    starts_cov = [None] * SEGS
    for group_index in range(GROUPS):
        mean_vec = end_mean[group_index]
        cov_mat = end_cov[group_index]
        for place_index in reversed(range(GROUP_SEGS)):
            segment = group_index * GROUP_SEGS + place_index
            ends_mean[segment] = mean_vec
            ends_cov[segment] = cov_mat
            mean_vec, cov_mat = apply_element(seg_gain[segment], seg_offset[segment], seg_noise[segment], mean_vec, cov_mat)
            starts_mean[segment] = mean_vec
            starts_cov[segment] = cov_mat
    start_cov = jnp.stack(starts_cov)
    start_mean = jnp.stack(starts_mean)
    inputs = (step_gain.reshape(SEGS, STEPS_SEG, D, D), step_offset.reshape(SEGS, STEPS_SEG, D), step_var.reshape(SEGS, STEPS_SEG, D), jnp.stack(ends_mean), jnp.stack(ends_cov))
    means, spread = lax.map(segment_moments, inputs)
    step_mean = means.reshape(STEPS, D)
    step_spread = spread.reshape(STEPS, D)
    tile_mean = step_mean.reshape(STEPS, NTILES, TILE_STATES)
    tile_spread = step_spread.reshape(STEPS, NTILES, TILE_STATES) + obs_noise.reshape(1, NTILES, TILE_STATES)
    onehot = (obs_tiles[:, :, None] == jnp.arange(NTILES, dtype=jnp.int32)[None, None, :]).astype(jnp.float32)
    picked_mean = jnp.einsum("ksn,kno->kso", onehot, tile_mean, precision=lax.Precision.HIGHEST)
    picked_spread = jnp.einsum("ksn,kno->kso", onehot, tile_spread, precision=lax.Precision.HIGHEST)
    live = jnp.arange(SLOTS, dtype=jnp.int32)[None, :] < obs_count[:, None]
    innovation = jnp.where(live[:, :, None], (obs_value - picked_mean) / picked_spread, jnp.float32(0.0))
    return start_cov, start_mean, step_mean, step_spread, innovation
```

```python
import jax
import jax.numpy as jnp
from jax import lax
from jax.experimental import pallas as pl
from jax.experimental.pallas import tpu as pltpu
from jax.sharding import PartitionSpec as P

MESH = pl.DeviceIdType.MESH
BF16 = jnp.bfloat16
F32 = jnp.float32
N = 1024
RB = 64
T = 128
NT = 8
KEEP = 5
SROWS = KEEP * RB + 16
GA, GB, S0, S1, GC = range(5)


def nn(x, y):
    return jnp.dot(x, y, preferred_element_type=F32)


def nt(x, y):
    return lax.dot_general(x, y, (((1,), (1,)), ((), ())), preferred_element_type=F32)


def mult(i, n):
    return pl.multiple_of(i * n, n)


def kernel(
    gain, off, noise, emean, ecov, sgain, soff, svar, otile, ocount, oval, onoise,
    o_cov, o_mean, o_sm, o_ss, o_in,
    ga, gb, gc, s0, s1, sp, a, x1, x2, d0, d1, dp, ps, rf, acc, xr, mrow, mhop, mb, covbuf, covsend,
    rr, sr, rc, sc, ini_s, ini_r, asem, esem, hop_s, hop_r, fwd_s, fwd_r, mv_s, mv_r, cv_s, cv_r, g_s, g_r,
):
    p = lax.axis_index("tm")
    z = lax.axis_index("tile")
    q = lax.rem(p, 4)
    c = lax.rem(p, 2)
    up = q // 2
    group = p // 4
    core_dev = (p + 1 - 2 * c, z)
    y_dev = (p + 2 - 4 * up, z)
    cross_dev = (p + 3 - 2 * q, z)
    right = (p, lax.rem(z + 1, 16))
    left = (p, lax.rem(z + 15, 16))
    tz = z // 2

    load_a = [
        pltpu.make_async_copy(sgain.at[k], a.at[pl.ds(k * RB, RB), :], asem.at[k]) for k in range(8)
    ]

    bar = pltpu.get_barrier_semaphore()
    for dev in (core_dev, y_dev, cross_dev, right, left):
        pl.semaphore_signal(bar, inc=1, device_id=dev, device_id_type=MESH)

    def ecopy(dd):
        j = mult(lax.rem(tz + dd, NT), T)
        return pltpu.make_async_copy(
            ecov.at[group, :, pl.ds(j, T)], s0.at[z, pl.ds(dd * RB, RB), :], esem.at[dd]
        )

    @pl.when(q == 2)
    def _():
        for dd in range(KEEP):
            ecopy(dd).start()

    def spread_row(row):
        zero = jnp.zeros_like(row)
        even = jnp.concatenate([row, zero], axis=1)
        odd = jnp.concatenate([zero, row], axis=1)
        return jnp.where(lax.rem(z, 2) == 0, even, odd)

    def vector_tile(hi, lo):
        which = lax.broadcasted_iota(jnp.int32, (16, T), 0)
        hi = jnp.broadcast_to(hi, (16, T))
        lo = jnp.broadcast_to(lo, (16, T))
        return jnp.where(which == 0, hi, jnp.where(which == 1, lo, 0.0)).astype(BF16)

    for dd in range(KEEP):
        j = mult(lax.rem(tz + dd, NT), T)
        sp[dd * RB : (dd + 1) * RB, :] = noise[0, :, pl.ds(j, T)]
    off_row = spread_row(off[...])
    off_hi = off_row.astype(BF16).astype(F32)
    sp[KEEP * RB :, :] = vector_tile(off_hi, off_row - off_hi)

    zrow = pl.ds(mult(z, RB), RB)

    @pl.when(c == 1)
    def _():
        ga[zrow, :] = gain[0]

    @pl.when(q == 0)
    def _():
        gc[zrow, :] = gain[0]

    @pl.when(q == 2)
    def _():
        rows = emean[...].astype(F32)
        pick = lax.broadcasted_iota(jnp.int32, rows.shape, 0) == group
        row = spread_row(jnp.sum(jnp.where(pick, rows, 0.0), axis=0, keepdims=True))
        s0[z, KEEP * RB :, :] = vector_tile(row, jnp.zeros_like(row))
        covsend[...] = gain[0]

    pl.semaphore_wait(bar, 5)

    def gat(buf):
        return lambda b: buf.at[pl.ds(mult(b, RB), RB), :]

    def sat(buf):
        return lambda b: buf.at[b]

    def rcopy(src, dst, ssem, rsem, dev):
        return pltpu.make_async_remote_copy(
            src_ref=src, dst_ref=dst, send_sem=ssem, recv_sem=rsem, device_id=dev, device_id_type=MESH
        )

    g2_copy = rcopy(covsend, gb.at[zrow, :], ini_s.at[0], ini_r.at[0], cross_dev)
    n2_copy = rcopy(sp, s1.at[z], ini_s.at[1], ini_r.at[1], y_dev)
    n3_copy = rcopy(sp, s1.at[z], ini_s.at[1], ini_r.at[1], core_dev)
    n1_copy = rcopy(sp, s0.at[z], ini_s.at[1], ini_r.at[2], core_dev)

    @pl.when(q == 3)
    def _():
        n3_copy.start()

    @pl.when(q == 1)
    def _():
        n1_copy.start()

    @pl.when(q == 2)
    def _():
        n2_copy.start()
        g2_copy.start()

    bufs = {GA: gat(ga), GB: gat(gb), S0: sat(s0), S1: sat(s1), GC: gat(gc)}

    def block(o):
        return lax.rem(z - o + 16, 16)

    def ring_send(item, o, ssem, to, dev):
        ref = bufs[item](block(o))
        return rcopy(ref, ref, ssem, rr.at[item, to], dev)

    def core_send(item, o):
        ref = bufs[item](block(o))
        return rcopy(ref, ref, sc.at[item, o], rc.at[item, o], core_dev)

    def ring_recv(item, o):
        ref = bufs[item](block(o))
        rcopy(ref, ref, sr.at[item, 0], rr.at[item, o], right).wait_recv()

    def start(item):
        ring_send(item, 0, sr.at[item, 0], 1, right).start()
        ring_send(item, 0, sr.at[item, 16], 15, left).start()
        if item != GC:
            core_send(item, 0).start()

    def step(item, k):
        ring_recv(item, k)
        ring_send(item, k, sr.at[item, k], k + 1, right).start()
        if item != GC:
            core_send(item, k).start()
        ring_recv(item, 16 - k)

        @pl.when(k < 7)
        def _():
            ring_send(item, 16 - k, sr.at[item, 16 - k], 15 - k, left).start()

        if item != GC:
            core_send(item, 16 - k).start()

    def last(item):
        ring_recv(item, 8)
        if item != GC:
            core_send(item, 8).start()

    def drain(item):
        def body(o, _):
            @pl.when((o != 8) & (o != 9))
            def _():
                ring_send(item, 0, sr.at[item, o], 1, right).wait_send()

            return 0

        lax.fori_loop(0, 17, body, 0)

        if item != GC:

            def body2(o, _):
                core_send(item, o).wait_send()
                return 0

            lax.fori_loop(0, 16, body2, 0)

    def core_recv(item):
        def body(o, _):
            core_send(item, o).wait_recv()
            return 0

        lax.fori_loop(0, 16, body, 0)

    @pl.when(c == 1)
    def _():
        start(GA)

        @pl.when(up == 0)
        def _():
            g2_copy.wait_recv()
            start(GB)

    @pl.when(c == 0)
    def _():
        @pl.when(up == 1)
        def _():
            for dd in range(KEEP):
                ecopy(dd).wait()
            start(S0)
            n3_copy.wait_recv()
            start(S1)

        @pl.when(up == 0)
        def _():
            n1_copy.wait_recv()
            start(S0)
            n2_copy.wait_recv()
            start(S1)
            start(GC)

    for cp in load_a:
        cp.start()

    def loop(k, _):
        @pl.when(c == 1)
        def _():
            step(GA, k)

            @pl.when(up == 0)
            def _():
                step(GB, k)

        @pl.when(c == 0)
        def _():
            step(S0, k)
            step(S1, k)

            @pl.when(up == 0)
            def _():
                step(GC, k)

        return 0

    lax.fori_loop(1, 8, loop, 0)

    @pl.when(c == 1)
    def _():
        last(GA)

        @pl.when(up == 0)
        def _():
            last(GB)

        core_recv(S0)
        core_recv(S1)

    @pl.when(c == 0)
    def _():
        last(S0)
        last(S1)
        core_recv(GA)

        @pl.when(up == 0)
        def _():
            core_recv(GB)

    for cp in load_a:
        cp.wait()

    def put(dense, t, dd, m):
        j = mult(lax.rem(t + dd, NT), T)
        t0 = mult(t, T)
        dense[pl.ds(t0, T), pl.ds(j, T)] = m
        if 1 <= dd <= 3:
            dense[pl.ds(j, T), pl.ds(t0, T)] = m.T

    def stile(s, t, dd):
        return jnp.concatenate(
            [s[2 * t, dd * RB : (dd + 1) * RB, :], s[2 * t + 1, dd * RB : (dd + 1) * RB, :]], axis=0
        )

    def unpack(s, dense):
        def body(t, _):
            for dd in range(KEEP):
                put(dense, t, dd, stile(s, t, dd))
            return 0

        lax.fori_loop(0, NT, body, 0)

    def unpack_state():
        def body(t, _):
            for dd in range(KEEP):
                put(dp, t, dd, ps[t, dd * T : (dd + 1) * T, :])
            return 0

        lax.fori_loop(0, NT, body, 0)

    def mm(x, y, out):
        def body(j, _):
            cols = pl.ds(mult(j, 256), 256)
            out[:, cols] = nn(x[...], y[:, cols]).astype(BF16)
            return 0

        lax.fori_loop(0, 4, body, 0)

    def quad(x, sym):
        def body(j, _):
            cols = pl.ds(mult(j, 256), 256)
            r = nn(x[...], sym[:, cols]) * x[:, cols].astype(F32)
            acc[...] += r[:, :T] + r[:, T:]
            return 0

        lax.fori_loop(0, 4, body, 0)

    def vec(s, row_count):
        parts = []
        for n in range(NT):
            tile = s[2 * n, KEEP * RB :, :].astype(F32) + s[2 * n + 1, KEEP * RB :, :].astype(F32)
            parts.append(tile)
        whole = jnp.concatenate(parts, axis=1)
        return whole[0:1, :] + whole[1:2, :] if row_count == 2 else whole[0:1, :]

    def set_mean(row):
        mrow[...] = jnp.broadcast_to(row, (16, N)).astype(BF16)

    def apply_mean(g, s):
        set_mean(nt(mrow[...], g[...])[0:1, :] + vec(s, 2))

    def step_means():
        r = nt(mrow[...], a[...])
        for k in range(8):
            o_sm[k : k + 1, :] = r[0:1, k * RB : (k + 1) * RB] + soff[k : k + 1, :]

    def own_mean():
        o_mean[...] = nt(mrow[...], gain[0])[0:1, :] + off[...]

    def finish_spread():
        row = jnp.sum(acc[...].T, axis=0, keepdims=True)
        for k in range(8):
            o_ss[k : k + 1, :] = row[:, k * RB : (k + 1) * RB] + svar[k : k + 1, :]

    def gather_copy(o):
        return rcopy(mb.at[z], mb.at[z], g_s.at[o], g_r.at[o], (p, lax.rem(z + o, 16)))

    def send_moments():
        mb[z] = jnp.concatenate([spread_row(o_sm[...]), spread_row(o_ss[...])], axis=0)

        def body(i, _):
            gather_copy(lax.rem(i + 7, 15) + 1).start()
            return 0

        lax.fori_loop(0, 15, body, 0)

    def hop_copy(t):
        return rcopy(ps.at[t], ps.at[t], hop_s.at[t], hop_r.at[t], y_dev)

    def fwd_copy(t):
        return rcopy(ps.at[t], ps.at[t], fwd_s.at[t], fwd_r.at[t], core_dev)

    mean_hop = rcopy(mrow, mhop, mv_s.at[0], mv_r.at[0], y_dev)
    cov_hop = rcopy(covsend, covbuf, cv_s.at[0], cv_r.at[0], cross_dev)
    other = (1 - c) * 4

    acc[...] = jnp.zeros_like(acc)

    @pl.when(up == 1)
    def _():
        unpack(s0, d0)
        half = pl.ds(mult(c, 512), 512)
        mm(ga.at[half, :], d0, x1)

        def body(i, _):
            t = c * 4 + i
            w = x1[pl.ds(mult(i, T), T), :]
            rf[...] = nt(w, ga[...])
            for dd in range(KEEP):
                j = mult(lax.rem(t + dd, NT), T)
                m = rf[:, pl.ds(j, T)] + stile(s1, t, dd).astype(F32)
                ps[t, dd * T : (dd + 1) * T, :] = m.astype(BF16)
            hop_copy(t).start()

            @pl.when(c == 1)
            def _():
                fwd_copy(t).start()

            return 0

        lax.fori_loop(0, 4, body, 0)
        set_mean(vec(s0, 1))

        @pl.when(q == 3)
        def _():
            step_means()
            own_mean()

        apply_mean(ga, s1)
        mean_hop.start()

        @pl.when(q == 3)
        def _():
            quad(a, d0)
            finish_spread()
            send_moments()
            mm(gain.at[0], d0, xr)
            o_cov[0] = (nt(xr[...], ga[...]) + noise[0].astype(F32)).astype(BF16)

        @pl.when(q == 2)
        def _():
            def rbody(i, _):
                fwd_copy(4 + i).wait_recv()
                return 0

            lax.fori_loop(0, 4, rbody, 0)
            unpack_state()
            step_means()
            own_mean()
            quad(a, dp)
            finish_spread()
            send_moments()
            cov_hop.wait_recv()
            o_cov[0] = covbuf[...]

    @pl.when(up == 0)
    def _():
        unpack(s1, d1)

        @pl.when(q == 1)
        def _():
            mm(a, gb, x1)
            quad(a, d1)

        @pl.when(q == 0)
        def _():
            unpack(s0, d0)
            mm(a, ga, x2)
            quad(a, d0)
            quad(x2, d1)
            mm(x2, gb, x1)

        def fbody(i, _):
            t = c * 4 + i
            hop_copy(t).wait_recv()
            fwd_copy(t).start()
            return 0

        lax.fori_loop(0, 4, fbody, 0)

        def gbody(i, _):
            fwd_copy(other + i).wait_recv()
            return 0

        lax.fori_loop(0, 4, gbody, 0)
        mean_hop.wait_recv()
        unpack_state()
        quad(x1, dp)
        finish_spread()
        mrow[...] = mhop[...]
        apply_mean(gb, s1)

        @pl.when(q == 0)
        def _():
            apply_mean(ga, s0)

        step_means()
        send_moments()
        own_mean()

        @pl.when(q == 1)
        def _():
            mm(gb.at[zrow, :], dp, xr)
            covsend[...] = (nt(xr[...], gb[...]) + d1[zrow, :].astype(F32)).astype(BF16)
            cov_hop.start()
            mm(gain.at[0], gb, xr)
            covbuf[...] = nn(xr[...], dp[...]).astype(BF16)
            xr[...] = (nt(covbuf[...], gb[...]) + nn(gain[0], d1[...])).astype(BF16)
            o_cov[0] = (nt(xr[...], ga[...]) + noise[0].astype(F32)).astype(BF16)
            cov_hop.wait_send()

        @pl.when(q == 0)
        def _():
            last(GC)
            mm(gain.at[0], ga, xr)
            mm(xr, gb, covbuf)
            covsend[...] = nn(covbuf[...], dp[...]).astype(BF16)
            covbuf[...] = (nt(covsend[...], gb[...]) + nn(xr[...], d1[...])).astype(BF16)
            xr[...] = (nt(covbuf[...], ga[...]) + nn(gain[0], d0[...])).astype(BF16)
            o_cov[0] = (nt(xr[...], gc[...]) + noise[0].astype(F32)).astype(BF16)

    @pl.when(c == 1)
    def _():
        drain(GA)
        n3_copy.wait_send()

        @pl.when(up == 0)
        def _():
            drain(GB)

    @pl.when(c == 0)
    def _():
        drain(S0)
        drain(S1)

        @pl.when(up == 0)
        def _():
            drain(GC)

    @pl.when(q == 2)
    def _():
        n2_copy.wait_send()
        g2_copy.wait_send()

    def sbody(i, _):
        t = c * 4 + i

        @pl.when(up == 1)
        def _():
            hop_copy(t).wait_send()

        @pl.when(q != 2)
        def _():
            fwd_copy(t).wait_send()

        return 0

    lax.fori_loop(0, 4, sbody, 0)

    @pl.when(up == 1)
    def _():
        mean_hop.wait_send()

    def wbody(o, _):
        ref = mb.at[block(o)]
        rcopy(ref, ref, g_s.at[o], g_r.at[o], right).wait_recv()
        return 0

    lax.fori_loop(1, 16, wbody, 0)
    picked_mean = [jnp.zeros((8, T), F32) for _ in range(4)]
    picked_spread = [jnp.zeros((8, T), F32) for _ in range(4)]
    for n in range(NT):
        tile = mb[2 * n] + mb[2 * n + 1]
        mean_n = tile[:8, :]
        spread_n = tile[8:, :] + onoise[n : n + 1, :]
        for j in range(4):
            hit = otile[:, j : j + 1] == n
            picked_mean[j] = jnp.where(hit, mean_n, picked_mean[j])
            picked_spread[j] = jnp.where(hit, spread_n, picked_spread[j])
    for j in range(4):
        value = (oval[:, j, :] - picked_mean[j]) / picked_spread[j]
        o_in[:, j, :] = jnp.where(ocount[...] > j, value, 0.0)

    def vbody(o, _):
        gather_copy(o).wait_send()
        return 0

    lax.fori_loop(1, 16, vbody, 0)


def shards(
    seg_gain, seg_offset, seg_noise, end_mean, end_cov, step_gain,
    step_offset, step_var, obs_tiles, obs_count, obs_value, obs_noise,
):
    vmem = pl.BlockSpec(memory_space=pltpu.VMEM)
    hbm = pl.BlockSpec(memory_space=pl.ANY)
    dma = pltpu.SemaphoreType.DMA
    out_cov, out_mean, step_mean, step_spread, innovation = pl.pallas_call(
        kernel,
        out_shape=(
            jax.ShapeDtypeStruct((1, RB, N), BF16),
            jax.ShapeDtypeStruct((1, RB), F32),
            jax.ShapeDtypeStruct((8, RB), F32),
            jax.ShapeDtypeStruct((8, RB), F32),
            jax.ShapeDtypeStruct((8, 4, T), F32),
        ),
        in_specs=[vmem, vmem, vmem, vmem, hbm, hbm, vmem, vmem, vmem, vmem, vmem, vmem],
        out_specs=(vmem,) * 5,
        scratch_shapes=[
            pltpu.VMEM((N, N), BF16),
            pltpu.VMEM((N, N), BF16),
            pltpu.VMEM((N, N), BF16),
            pltpu.VMEM((16, SROWS, T), BF16),
            pltpu.VMEM((16, SROWS, T), BF16),
            pltpu.VMEM((SROWS, T), BF16),
            pltpu.VMEM((512, N), BF16),
            pltpu.VMEM((512, N), BF16),
            pltpu.VMEM((512, N), BF16),
            pltpu.VMEM((N, N), BF16),
            pltpu.VMEM((N, N), BF16),
            pltpu.VMEM((N, N), BF16),
            pltpu.VMEM((NT, KEEP * T, T), BF16),
            pltpu.VMEM((T, N), F32),
            pltpu.VMEM((512, T), F32),
            pltpu.VMEM((RB, N), BF16),
            pltpu.VMEM((16, N), BF16),
            pltpu.VMEM((16, N), BF16),
            pltpu.VMEM((16, 16, T), F32),
            pltpu.VMEM((RB, N), BF16),
            pltpu.VMEM((RB, N), BF16),
            dma((5, 16)), dma((5, 17)), dma((5, 16)), dma((5, 16)),
            dma((2,)), dma((3,)), dma((8,)), dma((KEEP,)),
            dma((8,)), dma((8,)), dma((8,)), dma((8,)),
            dma((1,)), dma((1,)), dma((1,)), dma((1,)),
            dma((16,)), dma((16,)),
        ],
        compiler_params=pltpu.CompilerParams(
            collective_id=0, has_side_effects=True, vmem_limit_bytes=48 * 2**20
        ),
    )(
        seg_gain, seg_offset, seg_noise, end_mean, end_cov, step_gain,
        step_offset, step_var, obs_tiles, obs_count.reshape(8, 1), obs_value, obs_noise.reshape(NT, T),
    )
    return out_cov, out_mean.astype(BF16), step_mean, step_spread, innovation


def solution(mesh):
    in_specs = (
        P("tm", "tile", None), P("tm", "tile"), P("tm", "tile", None), P(None, "tile"),
        P(None, "tile", None), P("tm", "tile", None), P("tm", "tile"), P("tm", "tile"),
        P("tm", None), P("tm"), P("tm", None, None), P(),
    )
    out_specs = (
        P("tm", "tile", None), P("tm", "tile"), P("tm", "tile"), P("tm", "tile"), P("tm", None, None),
    )
    return jax.shard_map(shards, mesh=mesh, in_specs=in_specs, out_specs=out_specs, check_vma=False)
```

```python
import jax
import jax.numpy as jnp
from jax import lax
from jax.experimental import pallas as pl
from jax.experimental.pallas import tpu as pltpu
from jax.sharding import PartitionSpec as P

MESH = pl.DeviceIdType.MESH
BF16 = jnp.bfloat16
F32 = jnp.float32
N = 1024
RB = 64
T = 128
NT = 8
KEEP = 5
SROWS = KEEP * RB + 16
GA, GB, GC, S0, S1 = range(5)
CG = 2
CS = 2
NPARTS = 3 * CG + 2 * CS
PARTS = {i: tuple(range(i * CG, (i + 1) * CG)) for i in (GA, GB, GC)}
PARTS |= {i: tuple(range(3 * CG + (i - S0) * CS, 3 * CG + (i - S0 + 1) * CS)) for i in (S0, S1)}
S_CUTS = {1: ((0, SROWS),), 2: ((0, 176), (176, 160))}[CS]
LAG_B = 1
LAG_C = 2


def nn(x, y):
    return jnp.dot(x, y, preferred_element_type=F32)


def nt(x, y):
    return lax.dot_general(x, y, (((1,), (1,)), ((), ())), preferred_element_type=F32)


def mult(i, n):
    return pl.multiple_of(i * n, n)


def kernel(
    gain_h, off_h, noise_h, emean_h, ecov, sgain, soff_h, svar_h, otile_h, ocount_h, oval_h, onoise_h,
    o_cov, o_mean, o_sm, o_ss, o_in,
    ga, gb, gc, s0, s1, sp, a, x1, x2, d0, d1, dp, ps, rf, acc, mpre, xr, mrow, mhop, mb, covbuf, covsend,
    gain, off, noise, emean, soff, svar, otile, ocount, oval, onoise, lsem,
    rr, sr, rc, sc, ini_s, ini_r, asem, esem, hop_s, hop_r, fwd_s, fwd_r, mv_s, mv_r, cv_s, cv_r, g_s, g_r,
):
    p = lax.axis_index("tm")
    z = lax.axis_index("tile")
    q = lax.rem(p, 4)
    c = lax.rem(p, 2)
    up = q // 2
    group = p // 4
    core_dev = (p + 1 - 2 * c, z)
    y_dev = (p + 2 - 4 * up, z)
    cross_dev = (p + 3 - 2 * q, z)
    right = (p, lax.rem(z + 1, 16))
    left = (p, lax.rem(z + 15, 16))
    tz = z // 2

    load_a = [
        pltpu.make_async_copy(sgain.at[k], a.at[pl.ds(k * RB, RB), :], asem.at[k]) for k in range(8)
    ]

    pairs = (
        (gain_h, gain), (noise_h, noise), (off_h, off), (emean_h, emean), (soff_h, soff),
        (svar_h, svar), (otile_h, otile), (ocount_h, ocount), (oval_h, oval), (onoise_h, onoise),
    )
    loads = [pltpu.make_async_copy(src, dst, lsem.at[i]) for i, (src, dst) in enumerate(pairs)]

    bar = pltpu.get_barrier_semaphore()
    for dev in (core_dev, y_dev, cross_dev, right, left):
        pl.semaphore_signal(bar, inc=1, device_id=dev, device_id_type=MESH)

    def ecopy(dd):
        j = mult(lax.rem(tz + dd, NT), T)
        return pltpu.make_async_copy(
            ecov.at[group, :, pl.ds(j, T)], s0.at[z, pl.ds(dd * RB, RB), :], esem.at[dd]
        )

    @pl.when(q == 2)
    def _():
        for dd in range(KEEP):
            ecopy(dd).start()

    for cp in loads:
        cp.start()
    for cp in load_a:
        cp.start()
    for cp in loads[:4]:
        cp.wait()

    def spread_row(row):
        zero = jnp.zeros_like(row)
        even = jnp.concatenate([row, zero], axis=1)
        odd = jnp.concatenate([zero, row], axis=1)
        return jnp.where(lax.rem(z, 2) == 0, even, odd)

    def vector_tile(hi, lo):
        which = lax.broadcasted_iota(jnp.int32, (16, T), 0)
        hi = jnp.broadcast_to(hi, (16, T))
        lo = jnp.broadcast_to(lo, (16, T))
        return jnp.where(which == 0, hi, jnp.where(which == 1, lo, 0.0)).astype(BF16)

    for dd in range(KEEP):
        j = mult(lax.rem(tz + dd, NT), T)
        sp[dd * RB : (dd + 1) * RB, :] = noise[0, :, pl.ds(j, T)]
    off_row = spread_row(off[...])
    off_hi = off_row.astype(BF16).astype(F32)
    sp[KEEP * RB :, :] = vector_tile(off_hi, off_row - off_hi)

    zrow = pl.ds(mult(z, RB), RB)

    @pl.when(c == 1)
    def _():
        ga[zrow, :] = gain[0]

    @pl.when(q == 2)
    def _():
        rows = emean[...].astype(F32)
        pick = lax.broadcasted_iota(jnp.int32, rows.shape, 0) == group
        row = spread_row(jnp.sum(jnp.where(pick, rows, 0.0), axis=0, keepdims=True))
        s0[z, KEEP * RB :, :] = vector_tile(row, jnp.zeros_like(row))
        covsend[...] = gain[0]

    pl.semaphore_wait(bar, 5)

    def gat(buf):
        return lambda b: buf.at[pl.ds(mult(b, RB), RB), :]

    def sat(buf):
        return lambda b: buf.at[b]

    def rcopy(src, dst, ssem, rsem, dev):
        return pltpu.make_async_remote_copy(
            src_ref=src, dst_ref=dst, send_sem=ssem, recv_sem=rsem, device_id=dev, device_id_type=MESH
        )

    g2_copy = rcopy(covsend, gb.at[zrow, :], ini_s.at[0], ini_r.at[0], cross_dev)
    n2_copy = rcopy(sp, s1.at[z], ini_s.at[1], ini_r.at[1], y_dev)
    n3_copy = rcopy(sp, s1.at[z], ini_s.at[1], ini_r.at[1], core_dev)
    n1_copy = rcopy(sp, s0.at[z], ini_s.at[1], ini_r.at[2], core_dev)
    g0_copy = rcopy(gain.at[0], gc.at[zrow, :], ini_s.at[0], ini_r.at[1], core_dev)

    @pl.when(q == 3)
    def _():
        n3_copy.start()

    @pl.when(q == 1)
    def _():
        n1_copy.start()

    @pl.when(q == 0)
    def _():
        g0_copy.start()

    @pl.when(q == 2)
    def _():
        n2_copy.start()
        g2_copy.start()

    whole = {GA: gat(ga), GB: gat(gb), GC: gat(gc), S0: sat(s0), S1: sat(s1)}

    def piece(buf, i):
        rows = RB // CG
        return lambda b: buf.at[pl.ds(pl.multiple_of(b * RB + i * rows, rows), rows), :]

    def spiece(buf, i):
        return lambda b: buf.at[b, pl.ds(*S_CUTS[i]), :]

    bufs = [piece(g, i) for g in (ga, gb, gc) for i in range(CG)]
    bufs += [spiece(s, i) for s in (s0, s1) for i in range(CS)]

    def block(o):
        return lax.rem(z - o + 16, 16)

    def ring_send(part, o, ssem, to, dev):
        ref = bufs[part](block(o))
        return rcopy(ref, ref, ssem, rr.at[part, to], dev)

    def core_send(item, o):
        ref = whole[item](block(o))
        return rcopy(ref, ref, sc.at[item, o], rc.at[item, o], core_dev)

    def ring_recv(part, o):
        ref = bufs[part](block(o))
        rcopy(ref, ref, sr.at[part, 0], rr.at[part, o], right).wait_recv()

    def start(item):
        for part in PARTS[item]:
            ring_send(part, 0, sr.at[part, 0], 1, right).start()
            ring_send(part, 0, sr.at[part, 16], 15, left).start()
        core_send(item, 0).start()

    def step(item, k):
        for part in PARTS[item]:
            ring_recv(part, k)
            ring_send(part, k, sr.at[part, k], k + 1, right).start()
            ring_recv(part, 16 - k)

            @pl.when(k < 7)
            def _():
                ring_send(part, 16 - k, sr.at[part, 16 - k], 15 - k, left).start()

        core_send(item, k).start()
        core_send(item, 16 - k).start()

    def last(item):
        for part in PARTS[item]:
            ring_recv(part, 8)
        core_send(item, 8).start()

    def drain(item):
        for part in PARTS[item]:

            def body(o, _):
                @pl.when((o != 8) & (o != 9))
                def _():
                    ring_send(part, 0, sr.at[part, o], 1, right).wait_send()

                return 0

            lax.fori_loop(0, 17, body, 0)

        def body2(o, _):
            core_send(item, o).wait_send()
            return 0

        lax.fori_loop(0, 16, body2, 0)

    def core_recv(item):
        def body(o, _):
            core_send(item, o).wait_recv()
            return 0

        lax.fori_loop(0, 16, body, 0)

    def steps(lo, hi, *items):
        def body(k, _):
            for item, lag in items:
                step(item, k - lag)
            return 0

        lax.fori_loop(lo, hi, body, 0)

    @pl.when(q == 3)
    def _():
        start(GA)
        steps(1, 8, (GA, 0))
        last(GA)

    @pl.when(q == 2)
    def _():
        for dd in range(KEEP):
            ecopy(dd).wait()
        start(S0)
        n3_copy.wait_recv()
        start(S1)
        steps(1, 8, (S0, 0), (S1, 0))
        last(S0)
        last(S1)

    @pl.when(q == 1)
    def _():
        start(GA)
        steps(1, 1 + LAG_B, (GA, 0))
        g2_copy.wait_recv()
        start(GB)
        g0_copy.wait_recv()
        steps(1 + LAG_B, 1 + LAG_C, (GA, 0), (GB, LAG_B))
        start(GC)
        steps(1 + LAG_C, 8, (GA, 0), (GB, LAG_B), (GC, LAG_C))
        last(GA)
        steps(8, 8 + LAG_B, (GB, LAG_B), (GC, LAG_C))
        last(GB)

    @pl.when(q == 0)
    def _():
        n1_copy.wait_recv()
        start(S0)
        steps(1, 1 + LAG_B, (S0, 0))
        n2_copy.wait_recv()
        start(S1)
        steps(1 + LAG_B, 8, (S0, 0), (S1, LAG_B))
        last(S0)
        steps(8, 8 + LAG_B, (S1, LAG_B))
        last(S1)

    for cp in loads[4:]:
        cp.wait()
    for cp in load_a:
        cp.wait()

    def put(dense, t, dd, m):
        j = mult(lax.rem(t + dd, NT), T)
        t0 = mult(t, T)
        dense[pl.ds(t0, T), pl.ds(j, T)] = m
        if 1 <= dd <= 3:
            dense[pl.ds(j, T), pl.ds(t0, T)] = m.T

    def stile(s, t, dd):
        return jnp.concatenate(
            [s[2 * t, dd * RB : (dd + 1) * RB, :], s[2 * t + 1, dd * RB : (dd + 1) * RB, :]], axis=0
        )

    def unpack(s, dense):
        def body(t, _):
            for dd in range(KEEP):
                put(dense, t, dd, stile(s, t, dd))
            return 0

        lax.fori_loop(0, NT, body, 0)

    def put_state(t):
        for dd in range(KEEP):
            put(dp, t, dd, ps[t, dd * T : (dd + 1) * T, :])

    def mm_cols(x, y, out, j):
        cols = pl.ds(mult(j, 256), 256)
        out[:, cols] = nn(x[...], y[:, cols]).astype(BF16)

    def quad_cols(x, sym, j):
        cols = pl.ds(mult(j, 256), 256)
        r = nn(x[...], sym[:, cols]) * x[:, cols].astype(F32)
        acc[...] += r[:, :T] + r[:, T:]

    def mm(x, y, out):
        def body(j, _):
            mm_cols(x, y, out, j)
            return 0

        lax.fori_loop(0, 4, body, 0)

    def quad(x, sym):
        def body(j, _):
            quad_cols(x, sym, j)
            return 0

        lax.fori_loop(0, 4, body, 0)

    def vec_rows(s):
        parts = [s[2 * n, KEEP * RB :, :].astype(F32) + s[2 * n + 1, KEEP * RB :, :].astype(F32) for n in range(NT)]
        return jnp.concatenate(parts, axis=1).astype(BF16)

    def offset_part(s, x):
        r = nt(vec_rows(s), x[...])
        return r[0:1, :] + r[1:2, :]

    def vec(s, row_count):
        parts = []
        for n in range(NT):
            tile = s[2 * n, KEEP * RB :, :].astype(F32) + s[2 * n + 1, KEEP * RB :, :].astype(F32)
            parts.append(tile)
        whole = jnp.concatenate(parts, axis=1)
        return whole[0:1, :] + whole[1:2, :] if row_count == 2 else whole[0:1, :]

    def set_mean(row):
        mrow[...] = jnp.broadcast_to(row, (16, N)).astype(BF16)

    def apply_mean(g, s):
        set_mean(nt(mrow[...], g[...])[0:1, :] + vec(s, 2))

    def put_means(r):
        for k in range(8):
            o_sm[k : k + 1, :] = r[0:1, k * RB : (k + 1) * RB] + soff[k : k + 1, :]

    def step_means():
        put_means(nt(mrow[...], a[...])[0:1, :])

    def own_mean():
        o_mean[...] = nt(mrow[...], gain[0])[0:1, :] + off[...]

    def finish_spread():
        row = jnp.sum(acc[...].T, axis=0, keepdims=True)
        for k in range(8):
            o_ss[k : k + 1, :] = row[:, k * RB : (k + 1) * RB] + svar[k : k + 1, :]

    def gather_copy(o):
        return rcopy(mb.at[z], mb.at[z], g_s.at[o], g_r.at[o], (p, lax.rem(z + o, 16)))

    def send_moments():
        mb[z] = jnp.concatenate([spread_row(o_sm[...]), spread_row(o_ss[...])], axis=0)

        def body(i, _):
            gather_copy(lax.rem(i + 7, 15) + 1).start()
            return 0

        lax.fori_loop(0, 15, body, 0)

    def hop_copy(t):
        return rcopy(ps.at[t], ps.at[t], hop_s.at[t], hop_r.at[t], y_dev)

    def fwd_copy(t):
        return rcopy(ps.at[t], ps.at[t], fwd_s.at[t], fwd_r.at[t], core_dev)

    mean_hop = rcopy(mrow, mhop, mv_s.at[0], mv_r.at[0], y_dev)
    cov_hop = rcopy(covsend, covbuf, cv_s.at[0], cv_r.at[0], cross_dev)
    other = (1 - c) * 4

    acc[...] = jnp.zeros_like(acc)

    @pl.when(up == 1)
    def _():
        @pl.when(c == 1)
        def _():
            core_recv(S0)

        unpack(s0, d0)

        @pl.when(c == 0)
        def _():
            core_recv(GA)

        own_half = pl.ds(mult(c, 512), 512)
        mm(ga.at[own_half, :], d0, x1)

        @pl.when(c == 1)
        def _():
            core_recv(S1)

        def body(i, _):
            t = c * 4 + i
            w = x1[pl.ds(mult(i, T), T), :]
            rf[...] = nt(w, ga[...])
            for dd in range(KEEP):
                j = mult(lax.rem(t + dd, NT), T)
                m = rf[:, pl.ds(j, T)] + stile(s1, t, dd).astype(F32)
                ps[t, dd * T : (dd + 1) * T, :] = m.astype(BF16)
            hop_copy(t).start()

            @pl.when(c == 1)
            def _():
                fwd_copy(t).start()

            return 0

        lax.fori_loop(0, 4, body, 0)
        set_mean(vec(s0, 1))

        @pl.when(q == 3)
        def _():
            step_means()
            own_mean()

        apply_mean(ga, s1)
        mean_hop.start()

        @pl.when(q == 3)
        def _():
            quad(a, d0)
            finish_spread()
            send_moments()
            mm(gain.at[0], d0, xr)
            o_cov[0] = (nt(xr[...], ga[...]) + noise[0].astype(F32)).astype(BF16)

        @pl.when(q == 2)
        def _():
            def rbody(i, _):
                put_state(i)
                fwd_copy(4 + i).wait_recv()
                put_state(4 + i)
                return 0

            lax.fori_loop(0, 4, rbody, 0)
            step_means()
            own_mean()
            quad(a, dp)
            finish_spread()
            send_moments()
            cov_hop.wait_recv()
            o_cov[0] = covbuf[...]

    @pl.when(up == 0)
    def _():
        @pl.when(q == 1)
        def _():
            core_recv(S0)
            core_recv(S1)
            step(GC, 8 - LAG_C + LAG_B)
            unpack(s1, d1)

            def work(j, _):
                mm_cols(a, gb, x1, j)
                quad_cols(a, d1, j)

                @pl.when(j < LAG_C - LAG_B - 1)
                def _():
                    step(GC, 9 - LAG_C + LAG_B + j)

                return 0

            lax.fori_loop(0, 4, work, 0)
            last(GC)
            mpre[...] = offset_part(s1, a)

        @pl.when(q == 0)
        def _():
            unpack(s0, d0)
            core_recv(GA)
            mm(a, ga, x2)
            quad(a, d0)
            unpack(s1, d1)
            quad(x2, d1)
            core_recv(GB)
            mm(x2, gb, x1)
            mpre[...] = offset_part(s0, a) + offset_part(s1, x2)
            mm(gain.at[0], ga, xr)
            mm(xr, gb, covbuf)

        def fbody(i, _):
            t = c * 4 + i
            hop_copy(t).wait_recv()
            fwd_copy(t).start()
            put_state(t)
            return 0

        lax.fori_loop(0, 4, fbody, 0)

        def gbody(i, _):
            fwd_copy(other + i).wait_recv()
            put_state(other + i)
            return 0

        lax.fori_loop(0, 4, gbody, 0)
        quad(x1, dp)
        finish_spread()
        mean_hop.wait_recv()
        put_means(nt(mhop[...], x1[...])[0:1, :] + mpre[...])
        send_moments()
        mrow[...] = mhop[...]
        apply_mean(gb, s1)

        @pl.when(q == 0)
        def _():
            apply_mean(ga, s0)

        own_mean()

        @pl.when(q == 1)
        def _():
            mm(gb.at[zrow, :], dp, xr)
            covsend[...] = (nt(xr[...], gb[...]) + d1[zrow, :].astype(F32)).astype(BF16)
            cov_hop.start()
            mm(gain.at[0], gb, xr)
            covbuf[...] = nn(xr[...], dp[...]).astype(BF16)
            xr[...] = (nt(covbuf[...], gb[...]) + nn(gain[0], d1[...])).astype(BF16)
            o_cov[0] = (nt(xr[...], ga[...]) + noise[0].astype(F32)).astype(BF16)
            cov_hop.wait_send()

        @pl.when(q == 0)
        def _():
            covsend[...] = nn(covbuf[...], dp[...]).astype(BF16)
            covbuf[...] = (nt(covsend[...], gb[...]) + nn(xr[...], d1[...])).astype(BF16)
            xr[...] = (nt(covbuf[...], ga[...]) + nn(gain[0], d0[...])).astype(BF16)
            core_recv(GC)
            o_cov[0] = (nt(xr[...], gc[...]) + noise[0].astype(F32)).astype(BF16)

    @pl.when(c == 1)
    def _():
        drain(GA)
        n3_copy.wait_send()

        @pl.when(up == 0)
        def _():
            drain(GB)
            drain(GC)

    @pl.when(c == 0)
    def _():
        drain(S0)
        drain(S1)

        @pl.when(up == 0)
        def _():
            g0_copy.wait_send()

    @pl.when(q == 2)
    def _():
        n2_copy.wait_send()
        g2_copy.wait_send()

    def sbody(i, _):
        t = c * 4 + i

        @pl.when(up == 1)
        def _():
            hop_copy(t).wait_send()

        @pl.when(q != 2)
        def _():
            fwd_copy(t).wait_send()

        return 0

    lax.fori_loop(0, 4, sbody, 0)

    @pl.when(up == 1)
    def _():
        mean_hop.wait_send()

    def wbody(o, _):
        ref = mb.at[block(o)]
        rcopy(ref, ref, g_s.at[o], g_r.at[o], right).wait_recv()
        return 0

    lax.fori_loop(1, 16, wbody, 0)
    eye = lax.broadcasted_iota(jnp.int32, (8, 8), 0) == lax.broadcasted_iota(jnp.int32, (8, 8), 1)

    def column(row):
        return jnp.sum(jnp.where(eye, row.astype(F32), 0.0), axis=1, keepdims=True)

    tiles = [column(otile[j : j + 1, :]) for j in range(4)]
    counts = column(ocount[...])
    picked_mean = [jnp.zeros((8, T), F32) for _ in range(4)]
    picked_spread = [jnp.zeros((8, T), F32) for _ in range(4)]
    for n in range(NT):
        tile = mb[2 * n] + mb[2 * n + 1]
        mean_n = tile[:8, :]
        spread_n = tile[8:, :] + onoise[n : n + 1, :]
        for j in range(4):
            hit = tiles[j] == float(n)
            picked_mean[j] = jnp.where(hit, mean_n, picked_mean[j])
            picked_spread[j] = jnp.where(hit, spread_n, picked_spread[j])
    for j in range(4):
        value = (oval[:, j, :] - picked_mean[j]) / picked_spread[j]
        o_in[:, j, :] = jnp.where(counts > j + 0.5, value, 0.0)

    def vbody(o, _):
        gather_copy(o).wait_send()
        return 0

    lax.fori_loop(1, 16, vbody, 0)


def emit(cov, mean, sm, ss, inn, o_cov, o_mean, o_sm, o_ss, o_in):
    o_cov[...] = cov[...]
    o_mean[...] = mean[...].astype(BF16)
    o_sm[...] = sm[...]
    o_ss[...] = ss[...]
    o_in[...] = inn[...]


def shards(
    seg_gain, seg_offset, seg_noise, end_mean, end_cov, step_gain,
    step_offset, step_var, obs_tiles, obs_count, obs_value, obs_noise,
):
    vmem = pl.BlockSpec(memory_space=pltpu.VMEM)
    hbm = pl.BlockSpec(memory_space=pltpu.HBM)
    dma = pltpu.SemaphoreType.DMA
    out_cov, out_mean, step_mean, step_spread, innovation = pl.pallas_call(
        kernel,
        out_shape=(
            jax.ShapeDtypeStruct((1, RB, N), BF16),
            jax.ShapeDtypeStruct((1, RB), F32),
            jax.ShapeDtypeStruct((8, RB), F32),
            jax.ShapeDtypeStruct((8, RB), F32),
            jax.ShapeDtypeStruct((8, 4, T), F32),
        ),
        in_specs=[hbm] * 12,
        out_specs=(vmem,) * 5,
        scratch_shapes=[
            pltpu.VMEM((N, N), BF16),
            pltpu.VMEM((N, N), BF16),
            pltpu.VMEM((N, N), BF16),
            pltpu.VMEM((16, SROWS, T), BF16),
            pltpu.VMEM((16, SROWS, T), BF16),
            pltpu.VMEM((SROWS, T), BF16),
            pltpu.VMEM((512, N), BF16),
            pltpu.VMEM((512, N), BF16),
            pltpu.VMEM((512, N), BF16),
            pltpu.VMEM((N, N), BF16),
            pltpu.VMEM((N, N), BF16),
            pltpu.VMEM((N, N), BF16),
            pltpu.VMEM((NT, KEEP * T, T), BF16),
            pltpu.VMEM((T, N), F32),
            pltpu.VMEM((512, T), F32),
            pltpu.VMEM((1, 512), F32),
            pltpu.VMEM((RB, N), BF16),
            pltpu.VMEM((16, N), BF16),
            pltpu.VMEM((16, N), BF16),
            pltpu.VMEM((16, 16, T), F32),
            pltpu.VMEM((RB, N), BF16),
            pltpu.VMEM((RB, N), BF16),
            pltpu.VMEM((1, RB, N), BF16),
            pltpu.VMEM((1, RB), F32),
            pltpu.VMEM((1, RB, N), BF16),
            pltpu.VMEM((8, RB), BF16),
            pltpu.VMEM((8, RB), F32),
            pltpu.VMEM((8, RB), F32),
            pltpu.VMEM((4, 8), jnp.int32),
            pltpu.VMEM((1, 8), jnp.int32),
            pltpu.VMEM((8, 4, T), F32),
            pltpu.VMEM((NT, T), F32),
            dma((10,)),
            dma((NPARTS, 16)), dma((NPARTS, 17)), dma((5, 16)), dma((5, 16)),
            dma((2,)), dma((3,)), dma((8,)), dma((KEEP,)),
            dma((8,)), dma((8,)), dma((8,)), dma((8,)),
            dma((1,)), dma((1,)), dma((1,)), dma((1,)),
            dma((16,)), dma((16,)),
        ],
        compiler_params=pltpu.CompilerParams(
            collective_id=0, has_side_effects=True, vmem_limit_bytes=66 * 10**6
        ),
    )(
        seg_gain, seg_offset, seg_noise, end_mean, end_cov, step_gain,
        step_offset, step_var, obs_tiles.T, obs_count.reshape(1, 8), obs_value, obs_noise.reshape(NT, T),
    )
    return pl.pallas_call(
        emit,
        out_shape=(
            jax.ShapeDtypeStruct((1, RB, N), BF16),
            jax.ShapeDtypeStruct((1, RB), BF16),
            jax.ShapeDtypeStruct((8, RB), F32),
            jax.ShapeDtypeStruct((8, RB), F32),
            jax.ShapeDtypeStruct((8, 4, T), F32),
        ),
        in_specs=[vmem] * 5,
        out_specs=(vmem,) * 5,
    )(out_cov, out_mean, step_mean, step_spread, innovation)


def solution(mesh):
    in_specs = (
        P("tm", "tile", None), P("tm", "tile"), P("tm", "tile", None), P(None, "tile"),
        P(None, "tile", None), P("tm", "tile", None), P("tm", "tile"), P("tm", "tile"),
        P("tm", None), P("tm"), P("tm", None, None), P(),
    )
    out_specs = (
        P("tm", "tile", None), P("tm", "tile"), P("tm", "tile"), P("tm", "tile"), P("tm", None, None),
    )
    return jax.shard_map(shards, mesh=mesh, in_specs=in_specs, out_specs=out_specs, check_vma=False)
```

```python
import jax
import jax.numpy as jnp
from jax import lax
from jax.experimental import pallas as pl
from jax.experimental.pallas import tpu as pltpu
from jax.sharding import PartitionSpec as P

MESH = pl.DeviceIdType.MESH
BF16 = jnp.bfloat16
F32 = jnp.float32
N = 1024
RB = 64
T = 128
NT = 8
KEEP = 5
SROWS = KEEP * RB + 16
GA, GB, GC, S0, S1 = range(5)
CG = 2
CS = 2
NPARTS = 3 * CG + 2 * CS
PARTS = {i: tuple(range(i * CG, (i + 1) * CG)) for i in (GA, GB, GC)}
PARTS |= {i: tuple(range(3 * CG + (i - S0) * CS, 3 * CG + (i - S0 + 1) * CS)) for i in (S0, S1)}
S_CUTS = {1: ((0, SROWS),), 2: ((0, 176), (176, 160))}[CS]
LAG_B = 2
LAG_C = 4


def nn(x, y):
    return jnp.dot(x, y, preferred_element_type=F32)


def nt(x, y):
    return lax.dot_general(x, y, (((1,), (1,)), ((), ())), preferred_element_type=F32)


def mult(i, n):
    return pl.multiple_of(i * n, n)


def kernel(
    gain_h, off_h, noise_h, emean_h, ecov, sgain, soff_h, svar_h, otile_h, ocount_h, oval_h, onoise_h,
    o_cov, o_mean, o_sm, o_ss, o_in,
    ga, gb, gc, s0, s1, sp, a, x1, x2, d0, d1, dp, ps, rf, acc, mpre, xr, mrow, mhop, mb, covbuf, covsend,
    gain, off, noise, emean, soff, svar, otile, ocount, oval, onoise, lsem,
    rr, sr, rc, sc, ini_s, ini_r, asem, esem, hop_s, hop_r, fwd_s, fwd_r, mv_s, mv_r, cv_s, cv_r, g_s, g_r,
):
    p = lax.axis_index("tm")
    z = lax.axis_index("tile")
    q = lax.rem(p, 4)
    c = lax.rem(p, 2)
    up = q // 2
    group = p // 4
    core_dev = (p + 1 - 2 * c, z)
    y_dev = (p + 2 - 4 * up, z)
    cross_dev = (p + 3 - 2 * q, z)
    right = (p, lax.rem(z + 1, 16))
    left = (p, lax.rem(z + 15, 16))
    tz = z // 2

    load_a = [
        pltpu.make_async_copy(sgain.at[k], a.at[pl.ds(k * RB, RB), :], asem.at[k]) for k in range(8)
    ]

    pairs = (
        (gain_h, gain), (noise_h, noise), (off_h, off), (emean_h, emean), (soff_h, soff),
        (svar_h, svar), (otile_h, otile), (ocount_h, ocount), (oval_h, oval), (onoise_h, onoise),
    )
    loads = [pltpu.make_async_copy(src, dst, lsem.at[i]) for i, (src, dst) in enumerate(pairs)]

    bar = pltpu.get_barrier_semaphore()
    for dev in (core_dev, y_dev, cross_dev, right, left):
        pl.semaphore_signal(bar, inc=1, device_id=dev, device_id_type=MESH)

    def ecopy(dd):
        j = mult(lax.rem(tz + dd, NT), T)
        return pltpu.make_async_copy(
            ecov.at[group, :, pl.ds(j, T)], s0.at[z, pl.ds(dd * RB, RB), :], esem.at[dd]
        )

    @pl.when(q == 2)
    def _():
        for dd in range(KEEP):
            ecopy(dd).start()

    for cp in loads:
        cp.start()
    for cp in load_a:
        cp.start()
    for cp in loads[:4]:
        cp.wait()

    def spread_row(row):
        zero = jnp.zeros_like(row)
        even = jnp.concatenate([row, zero], axis=1)
        odd = jnp.concatenate([zero, row], axis=1)
        return jnp.where(lax.rem(z, 2) == 0, even, odd)

    def vector_tile(hi, lo):
        which = lax.broadcasted_iota(jnp.int32, (16, T), 0)
        hi = jnp.broadcast_to(hi, (16, T))
        lo = jnp.broadcast_to(lo, (16, T))
        return jnp.where(which == 0, hi, jnp.where(which == 1, lo, 0.0)).astype(BF16)

    for dd in range(KEEP):
        j = mult(lax.rem(tz + dd, NT), T)
        sp[dd * RB : (dd + 1) * RB, :] = noise[0, :, pl.ds(j, T)]
    off_row = spread_row(off[...])
    off_hi = off_row.astype(BF16).astype(F32)
    sp[KEEP * RB :, :] = vector_tile(off_hi, off_row - off_hi)

    zrow = pl.ds(mult(z, RB), RB)

    @pl.when(c == 1)
    def _():
        ga[zrow, :] = gain[0]

    @pl.when(q == 2)
    def _():
        rows = emean[...].astype(F32)
        pick = lax.broadcasted_iota(jnp.int32, rows.shape, 0) == group
        row = spread_row(jnp.sum(jnp.where(pick, rows, 0.0), axis=0, keepdims=True))
        s0[z, KEEP * RB :, :] = vector_tile(row, jnp.zeros_like(row))
        covsend[...] = gain[0]

    pl.semaphore_wait(bar, 5)

    def gat(buf):
        return lambda b: buf.at[pl.ds(mult(b, RB), RB), :]

    def sat(buf):
        return lambda b: buf.at[b]

    def rcopy(src, dst, ssem, rsem, dev):
        return pltpu.make_async_remote_copy(
            src_ref=src, dst_ref=dst, send_sem=ssem, recv_sem=rsem, device_id=dev, device_id_type=MESH
        )

    g2_copy = rcopy(covsend, gb.at[zrow, :], ini_s.at[0], ini_r.at[0], cross_dev)
    n2_copy = rcopy(sp, s1.at[z], ini_s.at[1], ini_r.at[1], y_dev)
    n3_copy = rcopy(sp, s1.at[z], ini_s.at[1], ini_r.at[1], core_dev)
    n1_copy = rcopy(sp, s0.at[z], ini_s.at[1], ini_r.at[2], core_dev)
    g0_copy = rcopy(gain.at[0], gc.at[zrow, :], ini_s.at[0], ini_r.at[1], core_dev)

    @pl.when(q == 3)
    def _():
        n3_copy.start()

    @pl.when(q == 1)
    def _():
        n1_copy.start()

    @pl.when(q == 0)
    def _():
        g0_copy.start()

    @pl.when(q == 2)
    def _():
        n2_copy.start()
        g2_copy.start()

    whole = {GA: gat(ga), GB: gat(gb), GC: gat(gc), S0: sat(s0), S1: sat(s1)}

    def piece(buf, i):
        rows = RB // CG
        return lambda b: buf.at[pl.ds(pl.multiple_of(b * RB + i * rows, rows), rows), :]

    def spiece(buf, i):
        return lambda b: buf.at[b, pl.ds(*S_CUTS[i]), :]

    bufs = [piece(g, i) for g in (ga, gb, gc) for i in range(CG)]
    bufs += [spiece(s, i) for s in (s0, s1) for i in range(CS)]

    def block(o):
        return lax.rem(z - o + 16, 16)

    def ring_send(part, o, ssem, to, dev):
        ref = bufs[part](block(o))
        return rcopy(ref, ref, ssem, rr.at[part, to], dev)

    def core_send(item, o):
        ref = whole[item](block(o))
        return rcopy(ref, ref, sc.at[item, o], rc.at[item, o], core_dev)

    def ring_recv(part, o):
        ref = bufs[part](block(o))
        rcopy(ref, ref, sr.at[part, 0], rr.at[part, o], right).wait_recv()

    def start(item):
        for part in PARTS[item]:
            ring_send(part, 0, sr.at[part, 0], 1, right).start()
            ring_send(part, 0, sr.at[part, 16], 15, left).start()
        core_send(item, 0).start()

    def step(item, k):
        for part in PARTS[item]:
            ring_recv(part, k)
            ring_send(part, k, sr.at[part, k], k + 1, right).start()
            ring_recv(part, 16 - k)

            @pl.when(k < 7)
            def _():
                ring_send(part, 16 - k, sr.at[part, 16 - k], 15 - k, left).start()

        core_send(item, k).start()
        core_send(item, 16 - k).start()

    def last(item):
        for part in PARTS[item]:
            ring_recv(part, 8)
        core_send(item, 8).start()

    def drain(item):
        for part in PARTS[item]:

            def body(o, _):
                @pl.when((o != 8) & (o != 9))
                def _():
                    ring_send(part, 0, sr.at[part, o], 1, right).wait_send()

                return 0

            lax.fori_loop(0, 17, body, 0)

        def body2(o, _):
            core_send(item, o).wait_send()
            return 0

        lax.fori_loop(0, 16, body2, 0)

    def core_recv(item):
        def body(o, _):
            core_send(item, o).wait_recv()
            return 0

        lax.fori_loop(0, 16, body, 0)

    def steps(lo, hi, *items):
        def body(k, _):
            for item, lag in items:
                step(item, k - lag)
            return 0

        lax.fori_loop(lo, hi, body, 0)

    @pl.when(q == 3)
    def _():
        start(GA)
        steps(1, 8, (GA, 0))
        last(GA)

    @pl.when(q == 2)
    def _():
        for dd in range(KEEP):
            ecopy(dd).wait()
        start(S0)
        n3_copy.wait_recv()
        start(S1)
        steps(1, 8, (S0, 0), (S1, 0))
        last(S0)
        last(S1)

    @pl.when(q == 1)
    def _():
        start(GA)
        steps(1, 1 + LAG_B, (GA, 0))
        g2_copy.wait_recv()
        start(GB)
        g0_copy.wait_recv()
        steps(1 + LAG_B, 1 + LAG_C, (GA, 0), (GB, LAG_B))
        start(GC)
        steps(1 + LAG_C, 8, (GA, 0), (GB, LAG_B), (GC, LAG_C))
        last(GA)
        steps(8, 8 + LAG_B, (GB, LAG_B), (GC, LAG_C))
        last(GB)

    @pl.when(q == 0)
    def _():
        n1_copy.wait_recv()
        start(S0)
        steps(1, 1 + LAG_B, (S0, 0))
        n2_copy.wait_recv()
        start(S1)
        steps(1 + LAG_B, 8, (S0, 0), (S1, LAG_B))
        last(S0)
        steps(8, 8 + LAG_B, (S1, LAG_B))
        last(S1)

    for cp in loads[4:]:
        cp.wait()
    for cp in load_a:
        cp.wait()

    def put(dense, t, dd, m):
        j = mult(lax.rem(t + dd, NT), T)
        t0 = mult(t, T)
        dense[pl.ds(t0, T), pl.ds(j, T)] = m
        if 1 <= dd <= 3:
            dense[pl.ds(j, T), pl.ds(t0, T)] = m.T

    def stile(s, t, dd):
        return jnp.concatenate(
            [s[2 * t, dd * RB : (dd + 1) * RB, :], s[2 * t + 1, dd * RB : (dd + 1) * RB, :]], axis=0
        )

    def unpack(s, dense):
        def body(t, _):
            for dd in range(KEEP):
                put(dense, t, dd, stile(s, t, dd))
            return 0

        lax.fori_loop(0, NT, body, 0)

    def put_state(t):
        for dd in range(KEEP):
            put(dp, t, dd, ps[t, dd * T : (dd + 1) * T, :])

    def mm_cols(x, y, out, j):
        cols = pl.ds(mult(j, 256), 256)
        out[:, cols] = nn(x[...], y[:, cols]).astype(BF16)

    def quad_cols(x, sym, j):
        cols = pl.ds(mult(j, 256), 256)
        r = nn(x[...], sym[:, cols]) * x[:, cols].astype(F32)
        acc[...] += r[:, :T] + r[:, T:]

    def mm(x, y, out):
        def body(j, _):
            mm_cols(x, y, out, j)
            return 0

        lax.fori_loop(0, 4, body, 0)

    def quad(x, sym):
        def body(j, _):
            quad_cols(x, sym, j)
            return 0

        lax.fori_loop(0, 4, body, 0)

    def vec_rows(s):
        parts = [s[2 * n, KEEP * RB :, :].astype(F32) + s[2 * n + 1, KEEP * RB :, :].astype(F32) for n in range(NT)]
        return jnp.concatenate(parts, axis=1).astype(BF16)

    def offset_part(s, x):
        r = nt(vec_rows(s), x[...])
        return r[0:1, :] + r[1:2, :]

    def vec(s, row_count):
        parts = []
        for n in range(NT):
            tile = s[2 * n, KEEP * RB :, :].astype(F32) + s[2 * n + 1, KEEP * RB :, :].astype(F32)
            parts.append(tile)
        whole = jnp.concatenate(parts, axis=1)
        return whole[0:1, :] + whole[1:2, :] if row_count == 2 else whole[0:1, :]

    def set_mean(row):
        mrow[...] = jnp.broadcast_to(row, (16, N)).astype(BF16)

    def apply_mean(g, s):
        set_mean(nt(mrow[...], g[...])[0:1, :] + vec(s, 2))

    def put_means(r):
        for k in range(8):
            o_sm[k : k + 1, :] = r[0:1, k * RB : (k + 1) * RB] + soff[k : k + 1, :]

    def step_means():
        put_means(nt(mrow[...], a[...])[0:1, :])

    def own_mean():
        o_mean[...] = nt(mrow[...], gain[0])[0:1, :] + off[...]

    def finish_spread():
        row = jnp.sum(acc[...].T, axis=0, keepdims=True)
        for k in range(8):
            o_ss[k : k + 1, :] = row[:, k * RB : (k + 1) * RB] + svar[k : k + 1, :]

    def gather_copy(o):
        return rcopy(mb.at[z], mb.at[z], g_s.at[o], g_r.at[o], (p, lax.rem(z + o, 16)))

    def send_moments():
        mb[z] = jnp.concatenate([spread_row(o_sm[...]), spread_row(o_ss[...])], axis=0)

        def body(i, _):
            gather_copy(lax.rem(i + 7, 15) + 1).start()
            return 0

        lax.fori_loop(0, 15, body, 0)

    def hop_copy(t):
        return rcopy(ps.at[t], ps.at[t], hop_s.at[t], hop_r.at[t], y_dev)

    def fwd_copy(t):
        return rcopy(ps.at[t], ps.at[t], fwd_s.at[t], fwd_r.at[t], core_dev)

    mean_hop = rcopy(mrow, mhop, mv_s.at[0], mv_r.at[0], y_dev)
    cov_hop = rcopy(covsend, covbuf, cv_s.at[0], cv_r.at[0], cross_dev)
    other = (1 - c) * 4

    acc[...] = jnp.zeros_like(acc)

    @pl.when(up == 1)
    def _():
        @pl.when(c == 1)
        def _():
            core_recv(S0)

        unpack(s0, d0)

        @pl.when(c == 0)
        def _():
            core_recv(GA)

        own_half = pl.ds(mult(c, 512), 512)
        mm(ga.at[own_half, :], d0, x1)

        @pl.when(c == 1)
        def _():
            core_recv(S1)

        def body(i, _):
            t = c * 4 + i
            w = x1[pl.ds(mult(i, T), T), :]
            rf[...] = nt(w, ga[...])
            for dd in range(KEEP):
                j = mult(lax.rem(t + dd, NT), T)
                m = rf[:, pl.ds(j, T)] + stile(s1, t, dd).astype(F32)
                ps[t, dd * T : (dd + 1) * T, :] = m.astype(BF16)
            hop_copy(t).start()

            @pl.when(c == 1)
            def _():
                fwd_copy(t).start()

            return 0

        lax.fori_loop(0, 4, body, 0)
        set_mean(vec(s0, 1))

        @pl.when(q == 3)
        def _():
            step_means()
            own_mean()

        apply_mean(ga, s1)
        mean_hop.start()

        @pl.when(q == 3)
        def _():
            quad(a, d0)
            finish_spread()
            send_moments()
            mm(gain.at[0], d0, xr)
            o_cov[0] = (nt(xr[...], ga[...]) + noise[0].astype(F32)).astype(BF16)

        @pl.when(q == 2)
        def _():
            def rbody(i, _):
                put_state(i)
                fwd_copy(4 + i).wait_recv()
                put_state(4 + i)
                return 0

            lax.fori_loop(0, 4, rbody, 0)
            step_means()
            own_mean()
            quad(a, dp)
            finish_spread()
            send_moments()
            cov_hop.wait_recv()
            o_cov[0] = covbuf[...]

    @pl.when(up == 0)
    def _():
        @pl.when(q == 1)
        def _():
            core_recv(S0)
            core_recv(S1)
            step(GC, 8 - LAG_C + LAG_B)
            unpack(s1, d1)

            def work(j, _):
                mm_cols(a, gb, x1, j)
                quad_cols(a, d1, j)

                @pl.when(j < LAG_C - LAG_B - 1)
                def _():
                    step(GC, 9 - LAG_C + LAG_B + j)

                return 0

            lax.fori_loop(0, 4, work, 0)
            last(GC)
            mpre[...] = offset_part(s1, a)

        @pl.when(q == 0)
        def _():
            unpack(s0, d0)
            core_recv(GA)
            mm(a, ga, x2)
            quad(a, d0)
            unpack(s1, d1)
            quad(x2, d1)
            core_recv(GB)
            mm(x2, gb, x1)
            mpre[...] = offset_part(s0, a) + offset_part(s1, x2)
            mm(gain.at[0], ga, xr)
            mm(xr, gb, covbuf)

        def fbody(i, _):
            t = c * 4 + i
            hop_copy(t).wait_recv()
            fwd_copy(t).start()
            put_state(t)
            return 0

        lax.fori_loop(0, 4, fbody, 0)

        def gbody(i, _):
            fwd_copy(other + i).wait_recv()
            put_state(other + i)
            return 0

        lax.fori_loop(0, 4, gbody, 0)
        quad(x1, dp)
        finish_spread()
        mean_hop.wait_recv()
        put_means(nt(mhop[...], x1[...])[0:1, :] + mpre[...])
        send_moments()
        mrow[...] = mhop[...]
        apply_mean(gb, s1)

        @pl.when(q == 0)
        def _():
            apply_mean(ga, s0)

        own_mean()

        @pl.when(q == 1)
        def _():
            mm(gb.at[zrow, :], dp, xr)
            covsend[...] = (nt(xr[...], gb[...]) + d1[zrow, :].astype(F32)).astype(BF16)
            cov_hop.start()
            mm(gain.at[0], gb, xr)
            covbuf[...] = nn(xr[...], dp[...]).astype(BF16)
            xr[...] = (nt(covbuf[...], gb[...]) + nn(gain[0], d1[...])).astype(BF16)
            o_cov[0] = (nt(xr[...], ga[...]) + noise[0].astype(F32)).astype(BF16)
            cov_hop.wait_send()

        @pl.when(q == 0)
        def _():
            covsend[...] = nn(covbuf[...], dp[...]).astype(BF16)
            covbuf[...] = (nt(covsend[...], gb[...]) + nn(xr[...], d1[...])).astype(BF16)
            xr[...] = (nt(covbuf[...], ga[...]) + nn(gain[0], d0[...])).astype(BF16)
            core_recv(GC)
            o_cov[0] = (nt(xr[...], gc[...]) + noise[0].astype(F32)).astype(BF16)

    @pl.when(c == 1)
    def _():
        drain(GA)
        n3_copy.wait_send()

        @pl.when(up == 0)
        def _():
            drain(GB)
            drain(GC)

    @pl.when(c == 0)
    def _():
        drain(S0)
        drain(S1)

        @pl.when(up == 0)
        def _():
            g0_copy.wait_send()

    @pl.when(q == 2)
    def _():
        n2_copy.wait_send()
        g2_copy.wait_send()

    def sbody(i, _):
        t = c * 4 + i

        @pl.when(up == 1)
        def _():
            hop_copy(t).wait_send()

        @pl.when(q != 2)
        def _():
            fwd_copy(t).wait_send()

        return 0

    lax.fori_loop(0, 4, sbody, 0)

    @pl.when(up == 1)
    def _():
        mean_hop.wait_send()

    def wbody(o, _):
        ref = mb.at[block(o)]
        rcopy(ref, ref, g_s.at[o], g_r.at[o], right).wait_recv()
        return 0

    lax.fori_loop(1, 16, wbody, 0)
    eye = lax.broadcasted_iota(jnp.int32, (8, 8), 0) == lax.broadcasted_iota(jnp.int32, (8, 8), 1)

    def column(row):
        return jnp.sum(jnp.where(eye, row.astype(F32), 0.0), axis=1, keepdims=True)

    tiles = [column(otile[j : j + 1, :]) for j in range(4)]
    counts = column(ocount[...])
    picked_mean = [jnp.zeros((8, T), F32) for _ in range(4)]
    picked_spread = [jnp.zeros((8, T), F32) for _ in range(4)]
    for n in range(NT):
        tile = mb[2 * n] + mb[2 * n + 1]
        mean_n = tile[:8, :]
        spread_n = tile[8:, :] + onoise[n : n + 1, :]
        for j in range(4):
            hit = tiles[j] == float(n)
            picked_mean[j] = jnp.where(hit, mean_n, picked_mean[j])
            picked_spread[j] = jnp.where(hit, spread_n, picked_spread[j])
    for j in range(4):
        value = (oval[:, j, :] - picked_mean[j]) / picked_spread[j]
        o_in[:, j, :] = jnp.where(counts > j + 0.5, value, 0.0)

    def vbody(o, _):
        gather_copy(o).wait_send()
        return 0

    lax.fori_loop(1, 16, vbody, 0)


def emit(cov, mean, sm, ss, inn, o_cov, o_mean, o_sm, o_ss, o_in):
    o_cov[...] = cov[...]
    o_mean[...] = mean[...].astype(BF16)
    o_sm[...] = sm[...]
    o_ss[...] = ss[...]
    o_in[...] = inn[...]


def shards(
    seg_gain, seg_offset, seg_noise, end_mean, end_cov, step_gain,
    step_offset, step_var, obs_tiles, obs_count, obs_value, obs_noise,
):
    vmem = pl.BlockSpec(memory_space=pltpu.VMEM)
    hbm = pl.BlockSpec(memory_space=pltpu.HBM)
    dma = pltpu.SemaphoreType.DMA
    out_cov, out_mean, step_mean, step_spread, innovation = pl.pallas_call(
        kernel,
        out_shape=(
            jax.ShapeDtypeStruct((1, RB, N), BF16),
            jax.ShapeDtypeStruct((1, RB), F32),
            jax.ShapeDtypeStruct((8, RB), F32),
            jax.ShapeDtypeStruct((8, RB), F32),
            jax.ShapeDtypeStruct((8, 4, T), F32),
        ),
        in_specs=[hbm] * 12,
        out_specs=(vmem,) * 5,
        scratch_shapes=[
            pltpu.VMEM((N, N), BF16),
            pltpu.VMEM((N, N), BF16),
            pltpu.VMEM((N, N), BF16),
            pltpu.VMEM((16, SROWS, T), BF16),
            pltpu.VMEM((16, SROWS, T), BF16),
            pltpu.VMEM((SROWS, T), BF16),
            pltpu.VMEM((512, N), BF16),
            pltpu.VMEM((512, N), BF16),
            pltpu.VMEM((512, N), BF16),
            pltpu.VMEM((N, N), BF16),
            pltpu.VMEM((N, N), BF16),
            pltpu.VMEM((N, N), BF16),
            pltpu.VMEM((NT, KEEP * T, T), BF16),
            pltpu.VMEM((T, N), F32),
            pltpu.VMEM((512, T), F32),
            pltpu.VMEM((1, 512), F32),
            pltpu.VMEM((RB, N), BF16),
            pltpu.VMEM((16, N), BF16),
            pltpu.VMEM((16, N), BF16),
            pltpu.VMEM((16, 16, T), F32),
            pltpu.VMEM((RB, N), BF16),
            pltpu.VMEM((RB, N), BF16),
            pltpu.VMEM((1, RB, N), BF16),
            pltpu.VMEM((1, RB), F32),
            pltpu.VMEM((1, RB, N), BF16),
            pltpu.VMEM((8, RB), BF16),
            pltpu.VMEM((8, RB), F32),
            pltpu.VMEM((8, RB), F32),
            pltpu.VMEM((4, 8), jnp.int32),
            pltpu.VMEM((1, 8), jnp.int32),
            pltpu.VMEM((8, 4, T), F32),
            pltpu.VMEM((NT, T), F32),
            dma((10,)),
            dma((NPARTS, 16)), dma((NPARTS, 17)), dma((5, 16)), dma((5, 16)),
            dma((2,)), dma((3,)), dma((8,)), dma((KEEP,)),
            dma((8,)), dma((8,)), dma((8,)), dma((8,)),
            dma((1,)), dma((1,)), dma((1,)), dma((1,)),
            dma((16,)), dma((16,)),
        ],
        compiler_params=pltpu.CompilerParams(
            collective_id=0, has_side_effects=True, vmem_limit_bytes=66 * 10**6
        ),
    )(
        seg_gain, seg_offset, seg_noise, end_mean, end_cov, step_gain,
        step_offset, step_var, obs_tiles.T, obs_count.reshape(1, 8), obs_value, obs_noise.reshape(NT, T),
    )
    return pl.pallas_call(
        emit,
        out_shape=(
            jax.ShapeDtypeStruct((1, RB, N), BF16),
            jax.ShapeDtypeStruct((1, RB), BF16),
            jax.ShapeDtypeStruct((8, RB), F32),
            jax.ShapeDtypeStruct((8, RB), F32),
            jax.ShapeDtypeStruct((8, 4, T), F32),
        ),
        in_specs=[vmem] * 5,
        out_specs=(vmem,) * 5,
    )(out_cov, out_mean, step_mean, step_spread, innovation)


def solution(mesh):
    in_specs = (
        P("tm", "tile", None), P("tm", "tile"), P("tm", "tile", None), P(None, "tile"),
        P(None, "tile", None), P("tm", "tile", None), P("tm", "tile"), P("tm", "tile"),
        P("tm", None), P("tm"), P("tm", None, None), P(),
    )
    out_specs = (
        P("tm", "tile", None), P("tm", "tile"), P("tm", "tile"), P("tm", "tile"), P("tm", None, None),
    )
    return jax.shard_map(shards, mesh=mesh, in_specs=in_specs, out_specs=out_specs, check_vma=False)
```
